32 devices in a mesh: groups: 2 (over y), expert: 4 (over z), dp: 4 (over x, core).
Axes of the slice: x: 2, y: 2, z: 4, core: 2. Of those that a mesh axis runs over, the one named last changes fastest.
Arguments:
- inputs: bfloat16 [1024, 7168], P(('groups', 'expert', 'dp')), parts along dimension 0, may hold values from -6 to 6
- out_grads: bfloat16 [1024, 8, 2048], P(('groups', 'expert', 'dp')), parts along dimension 0, may hold values from -6 to 6
- routing: int32 [1024, 8], P(('groups', 'expert', 'dp')), parts along dimension 0, may hold values from 0 to 31, all different within a row; in each aligned block of 32 rows (0 to 31, 32 to 63, ...) at most 16 rows name the same one
- in_basis: bfloat16 [7168, 64], replicated, may hold values from -0.0625 to 0.0625
- out_basis: bfloat16 [32, 2048, 64], P('expert'), may hold values from -0.125 to 0.125
- val_bank: bfloat16 [256, 4096], P(('groups', 'dp')), parts along dimension 0, may hold values from -0.03125 to 0.03125
- val_ids: int32 [512], P('groups'), parts along dimension 0, may hold values from 0 to 127
Outputs:
- scores: float32 [1024, 256], P(('groups', 'expert', 'dp')), parts along dimension 0
The draws below stay inside these ranges and needn't reach their ends.
There are 2 independent parts, one for each index of `groups`. The reference program is written for one: setup_inputs(seed, part) draws one part's arguments, and reference() takes and returns one part's arrays. A program takes and returns all parts, laid end to end along the dimension named above; an argument that names none is the same for every part. Nothing has to cross between parts.
Inputs may be any that keep to these rules, and one draw needn't show every extreme that they name: `routing`: each token names 8 different experts; among the 32 tokens of one device no expert is named by more than 16 tokens, a bound that some block reaches.
All inputs are finite; a program needn't handle non-finite values.
Results may differ from the reference program's by a relative error of at most 0.0051.
Values may be sent and summed in bfloat16 or wider, within the bound.
A program may use at most 64 MiB of HBM per device.

```python
import math
import jax
import jax.numpy as jnp
import numpy as np
from jax import lax

D = 7168
FF = 2048
TOPK = 8
RANK = 64
TOK_DEV = 32
NVAL = 256
EXPERTS = 32
TOKENS = 512
NBANK = 128
MOST = 16


def with_ends(entries, rng, least, top_value):
    dims = entries.shape
    index_at = [jax.random.randint(jax.random.fold_in(rng, axis), (), 0, dims[axis]) for axis in range(len(dims))]
    entries = entries.at[tuple(index_at)].set(least)
    longest = dims.index(max(dims))
    index_at[longest] = (index_at[longest] + 1) % dims[longest]
    return entries.at[tuple(index_at)].set(top_value)


def levels(key, dims, pieces, smallest, top_value):
    factor_of, own = 1.0, jax.random.fold_in(key, 6)
    for position, parts in pieces:
        draws = jnp.exp(jax.random.uniform(jax.random.fold_in(own, position), (parts,), jnp.float32, smallest / len(pieces), top_value / len(pieces)))
        factor_of = factor_of * jnp.repeat(draws, dims[position] // parts).reshape([-1 if axis == position else 1 for axis in range(len(dims))])
    return factor_of


def shared_out(key, own, number, rows, count, top, reach, lean):
    order = jax.random.permutation(key, count)
    packed, common = portions_of(count, rows * top, reach, lean, True), portions_of(count, rows * top, reach, lean, False)
    places = jnp.arange(count)

    def named(sizes, turn):
        used = int((sizes > 0).sum())
        fixed = max(1, used // 4)
        passed = fixed + (places - fixed + turn * (used - fixed)) % max(1, count - fixed)
        return jnp.zeros((count,), jnp.int32).at[order[jnp.where(places < fixed, places, passed)]].set(jnp.asarray(sizes, jnp.int32))

    sizes = jnp.where(number % 4 == 0, named(packed, number // 4), named(common, number - number // 4 - 1))
    mixed = jax.random.permutation(jax.random.fold_in(own, 3), count)
    giver, receiver = mixed[0:count // 2 * 2:2], mixed[1:count // 2 * 2:2]
    margin = jnp.minimum(sizes[giver] - 1, reach - sizes[receiver]) // 2
    margin = jnp.where((giver == order[0]) | (receiver == order[0]) | (sizes[receiver] == 0), 0, jnp.maximum(margin, 0))
    passed = jax.random.randint(jax.random.fold_in(own, 4), (count // 2,), 0, 1 << 20) % (margin + 1)
    sizes = sizes.at[giver].add(-passed).at[receiver].add(passed)
    labels = jnp.searchsorted(jnp.cumsum(sizes), jnp.arange(rows * top), side="right").astype(jnp.int32)
    listing = labels.reshape(top, rows).T
    listing = listing[jax.random.permutation(jax.random.fold_in(own, 1), rows)]
    turn = jax.random.randint(jax.random.fold_in(own, 2), (rows, 1), 0, top)
    return jnp.take_along_axis(listing, (jnp.arange(top)[None, :] + turn) % top, axis=1)


def portions_of(amount, total, reach, skew, full):
    loads = [(1 << 20) // math.isqrt(rank ** skew) + 1 for rank in range(1, amount + 1)]
    largest = reach if full else min(reach, max(-(-total // amount), total * loads[0] // sum(loads)))
    least = 1 if total - largest >= amount - 1 else 0
    given, rest = [largest] + [least] * (amount - 1), total - largest - least * (amount - 1)
    while rest > 0:
        candidates = [i for i in range(1, amount) if given[i] < largest] or [i for i in range(1, amount) if given[i] < reach]
        whole, budget = sum([loads[i] for i in candidates]), rest
        for i in candidates:
            more = min(reach - given[i], max(1, budget * loads[i] // whole), rest)
            given[i] = given[i] + more
            rest = rest - more
    return np.array(given)


def noise(rng, shape, deviation, limit, pieces=(), dtype=jnp.bfloat16):
    values = deviation * jax.random.normal(rng, shape, jnp.float32)
    if pieces:
        values = values * levels(rng, shape, pieces, -0.22, 0.18)
    return jnp.clip(values, -limit, limit).astype(dtype)


def setup_inputs(seed: int = 0, part: int = 0) -> dict:
    streams_of = jax.random.split(jax.random.key(seed), 8)
    part_splits = jax.random.split(jax.random.fold_in(streams_of[7], part), 8)
    inputs = noise(part_splits[0], (TOKENS, D), 1.0, 6.0, ((0, 16),))
    out_grads = noise(part_splits[1], (TOKENS, TOPK, FF), 1.0, 6.0, ((0, 16),))
    routing_keys = jax.random.split(jax.random.fold_in(part_splits[2], 1), TOKENS // TOK_DEV)
    routing_turns = jax.random.permutation(jax.random.fold_in(part_splits[2], 3), TOKENS // TOK_DEV)
    routing = jax.vmap(lambda own, number: shared_out(jax.random.fold_in(part_splits[2], 2), own, number, TOK_DEV, EXPERTS, TOPK, MOST, 2))(routing_keys, routing_turns).reshape((TOKENS, TOPK))
    in_basis = noise(streams_of[3], (D, RANK), D ** -0.5, 0.0625)
    out_basis = noise(streams_of[4], (EXPERTS, FF, RANK), FF ** -0.5, 0.125, ((0, 4),))
    val_bank = noise(part_splits[5], (NBANK, RANK * RANK), (8 * RANK * RANK) ** -0.5, 0.03125, ((0, 4),))
    val_ids = with_ends(jax.random.randint(part_splits[6], (NVAL,), 0, NBANK), jax.random.fold_in(part_splits[6], 1), 0, NBANK - 1).astype(jnp.int32)
    return dict(inputs=inputs, out_grads=out_grads, routing=routing, in_basis=in_basis, out_basis=out_basis, val_bank=val_bank, val_ids=val_ids)


def reference(inputs, out_grads, routing, in_basis, out_basis, val_bank, val_ids):
    blocks = TOKENS // TOK_DEV

    def one_block(operands):
        rows_in, grads_in, routes_in = operands
        left_proj = jnp.dot(rows_in, in_basis, preferred_element_type=jnp.float32).astype(jnp.bfloat16)
        left_wide = left_proj.astype(jnp.float32)
        chosen = out_basis[routes_in.reshape(-1)].astype(jnp.float32)
        right_proj = jnp.einsum("pf,pfr->pr", grads_in.reshape(-1, FF).astype(jnp.float32), chosen)
        right_proj = right_proj.reshape(TOK_DEV, TOPK, RANK)
        pair_sketch = (left_wide[:, None, :, None] * right_proj[:, :, None, :]).astype(jnp.bfloat16)
        pair_sketch = lax.optimization_barrier(pair_sketch)
        summed = jnp.sum(pair_sketch.astype(jnp.float32), axis=1)
        return summed.reshape(TOK_DEV, RANK * RANK).astype(jnp.bfloat16)

    sketch = lax.map(one_block, (inputs.reshape(blocks, TOK_DEV, D),
                                 out_grads.reshape(blocks, TOK_DEV, TOPK, FF),
                                 routing.reshape(blocks, TOK_DEV, TOPK)))
    sketch = sketch.reshape(TOKENS, RANK * RANK)
    bank_scores = jnp.dot(sketch, val_bank.T, preferred_element_type=jnp.float32)
    return bank_scores[:, val_ids.astype(jnp.int32)]
```

```python
import functools

import jax
import jax.numpy as jnp
from jax import lax
from jax.experimental import pallas as pl
from jax.experimental.pallas import tpu as pltpu
from jax.sharding import PartitionSpec as P

F32, BF16, I32 = jnp.float32, jnp.bfloat16, jnp.int32
MESH = pl.DeviceIdType.MESH
NT = (((1,), (1,)), ((), ()))
TN = (((0,), (0,)), ((), ()))
CHUNKS = 2


def flip(index, mask):
    result, bit = index, 1
    while bit <= mask:
        if mask & bit:
            result = result + bit * (1 - 2 * ((index // bit) % 2))
        bit *= 2
    return result


def kernel(
    sizes, x_ref, inb_ref, og_ref, rt_ref, wt_ref, bank_ref, ids_ref, out_ref,
    xbuf, ibuf, gbuf, wbuf, rbuf, rq, acc, psend, pbuf, bbuf, bsel, lrep,
    g_send, g_recv, r_send, r_recv, p_send, p_recv, b_send, b_recv,
    wr_send, wl_send, w_recv, local_sem,
):
    groups, owners, dps, topk, experts, rank = sizes
    plane = groups * dps
    tokens = x_ref.shape[0]
    pairs = og_ref.shape[0]
    width = gbuf.shape[2]
    rows = wt_ref.shape[0] // CHUNKS
    per_chunk = experts // CHUNKS
    half_tokens = tokens // 2
    g, z, d = lax.axis_index("groups"), lax.axis_index("expert"), lax.axis_index("dp")
    me = g * dps + d
    last = owners - 1

    def place(q):
        return {"groups": q // dps, "dp": q % dps}

    barrier = pltpu.get_barrier_semaphore()
    for r in range(1, plane):
        pl.semaphore_signal(barrier, inc=1, device_id=place((me + r) % plane), device_id_type=MESH)

    @pl.when(z > 0)
    def _():
        pl.semaphore_signal(barrier, inc=1, device_id={"expert": z - 1}, device_id_type=MESH)

    @pl.when(z < last)
    def _():
        pl.semaphore_signal(barrier, inc=1, device_id={"expert": z + 1}, device_id_type=MESH)

    def slice_of(q):
        return pl.ds(pl.multiple_of(q * width, width), width)

    local = [
        pltpu.make_async_copy(x_ref, xbuf, local_sem.at[0]),
        pltpu.make_async_copy(inb_ref, ibuf, local_sem.at[1]),
        pltpu.make_async_copy(og_ref.at[:, slice_of(me)], gbuf.at[me], local_sem.at[2]),
        pltpu.make_async_copy(wt_ref.at[:, slice_of(me)], wbuf.at[z], local_sem.at[3]),
        pltpu.make_async_copy(bank_ref, bbuf.at[d], local_sem.at[4]),
    ]
    for copy in local:
        copy.start()
    rbuf[me] = jnp.zeros(rbuf.shape[1:], F32)
    rbuf[me, :, :tokens] = rt_ref[...].astype(F32)

    def w_copy(source, s, c, to, sems):
        return pltpu.make_async_remote_copy(
            src_ref=source,
            dst_ref=wbuf.at[s, pl.ds(c * rows, rows)],
            send_sem=sems.at[s * CHUNKS + c],
            recv_sem=w_recv.at[s * CHUNKS + c],
            device_id={"expert": to},
            device_id_type=MESH,
        )

    def w_passed(s, c, to, sems):
        return w_copy(wbuf.at[s, pl.ds(c * rows, rows)], s, c, to, sems)

    def g_copy(q, r):
        return pltpu.make_async_remote_copy(
            src_ref=og_ref.at[:, slice_of(q)], dst_ref=gbuf.at[me],
            send_sem=g_send.at[r], recv_sem=g_recv.at[r],
            device_id=place(q), device_id_type=MESH,
        )

    def r_copy(q, r):
        return pltpu.make_async_remote_copy(
            src_ref=rbuf.at[me], dst_ref=rbuf.at[me],
            send_sem=r_send.at[r], recv_sem=r_recv.at[r],
            device_id=place(q), device_id_type=MESH,
        )

    def p_copy(q, r):
        return pltpu.make_async_remote_copy(
            src_ref=psend.at[q], dst_ref=pbuf.at[me],
            send_sem=p_send.at[r], recv_sem=p_recv.at[r],
            device_id=place(q), device_id_type=MESH,
        )

    bits = []
    bit = dps // 2
    while bit:
        bits.append(bit)
        bit //= 2
    b_copies = []

    def b_copy(source, shard, bit):
        copy = pltpu.make_async_remote_copy(
            src_ref=source, dst_ref=bbuf.at[shard],
            send_sem=b_send.at[len(b_copies)], recv_sem=b_recv.at[shard],
            device_id={"dp": flip(d, bit)}, device_id_type=MESH,
        )
        b_copies.append(copy)
        return copy

    def b_wait(shard):
        pltpu.make_async_remote_copy(
            src_ref=bbuf.at[shard], dst_ref=bbuf.at[shard],
            send_sem=b_send.at[0], recv_sem=b_recv.at[shard],
            device_id={"dp": flip(d, 1)}, device_id_type=MESH,
        ).wait_recv()

    pl.semaphore_wait(barrier, plane - 1 + jnp.where(z > 0, 1, 0) + jnp.where(z < last, 1, 0))

    for c in range(CHUNKS):
        own = wt_ref.at[pl.ds(c * rows, rows), slice_of(me)]

        @pl.when(z > 0)
        def _(own=own, c=c):
            w_copy(own, z, c, z - 1, wl_send).start()

        @pl.when(z < last)
        def _(own=own, c=c):
            w_copy(own, z, c, z + 1, wr_send).start()

    for r in range(1, plane):
        g_copy((me + r) % plane, r).start()
        r_copy((me + r) % plane, r).start()
    for bit in bits:
        b_copy(bank_ref, d, bit).start()

    local[0].wait()
    local[1].wait()
    left = lax.dot_general(xbuf[...], ibuf[...], NT, preferred_element_type=F32)
    left = left.astype(BF16).astype(F32)
    low = lax.broadcasted_iota(I32, (tokens, 2 * rank), 1) < rank
    for i in range(rank // 2):
        lrep[:, i * 2 * rank:(i + 1) * 2 * rank] = jnp.where(
            low, left[:, 2 * i:2 * i + 1], left[:, 2 * i + 1:2 * i + 2]
        )
    acc[...] = jnp.zeros_like(acc)

    @pl.when(jnp.logical_and(z > 0, z < last))
    def _():
        def step(i, carry):
            j, c = i // CHUNKS, i % CHUNKS

            @pl.when(z - 1 - j >= 0)
            def _():
                copy = w_passed(z - 1 - j, c, z + 1, wr_send)
                copy.wait_recv()
                copy.start()

            @pl.when(z + 1 + j <= last)
            def _():
                copy = w_passed(z + 1 + j, c, z - 1, wl_send)
                copy.wait_recv()
                copy.start()

            return carry

        lax.fori_loop(0, (owners - 2) * CHUNKS, step, 0)

    for r in range(1, plane):
        r_copy((me + r) % plane, r).wait_recv()
    shift, mask = topk.bit_length() - 1, topk - 1
    spread = (
        lax.broadcasted_iota(I32, (pairs, rbuf.shape[2]), 0) >> shift
        == lax.broadcasted_iota(I32, (pairs, rbuf.shape[2]), 1)
    ).astype(F32).astype(BF16)
    mine = (
        lax.broadcasted_iota(I32, (pairs, topk), 0) & mask
        == lax.broadcasted_iota(I32, (pairs, topk), 1)
    )
    half = (lax.broadcasted_iota(I32, (pairs, 2 * rank), 1) >= rank).astype(F32)

    def routes(q, carry):
        named = lax.dot_general(spread, rbuf[q].astype(BF16), NT, preferred_element_type=F32)
        named = jnp.sum(jnp.where(mine, named, 0.0), axis=1, keepdims=True)
        rq[q] = named - half
        return carry

    lax.fori_loop(0, plane, routes, 0)

    masks = [m for b in bits for m in range(1, dps) if m & -m == b]
    for m in masks:
        b_wait(flip(d, m))
        for bit in bits:
            if bit < (m & -m):
                b_copy(bbuf.at[flip(d, m)], flip(d, m), bit).start()
    local[4].wait()
    bank_rows = dps * bank_ref.shape[0]
    select = (
        lax.broadcasted_iota(I32, (bank_rows, ids_ref.shape[1]), 0) == ids_ref[...]
    ).astype(F32).astype(BF16)
    cut = 512

    def choose(i, carry):
        columns = pl.ds(pl.multiple_of(i * cut, cut), cut)
        whole = bbuf[:, :, columns].reshape(bank_rows, cut)
        bsel[:, columns] = lax.dot_general(
            select, whole, TN, preferred_element_type=F32
        ).astype(BF16)
        return carry

    lax.fori_loop(0, bsel.shape[1] // cut, choose, 0)

    for r in range(1, plane):
        g_copy((me + r) % plane, r).wait_recv()
    local[2].wait()
    local[3].wait()

    near = jnp.minimum(z, last - z)
    far_sign = jnp.where(z < last - z, 1, -1)

    def shard_at(j):
        paired = j <= 2 * near
        distance = jnp.where(paired, (j + 1) // 2, j - near)
        sign = jnp.where(paired, 1 - 2 * (j % 2), far_sign)
        return z + sign * distance

    at_end = jnp.logical_or(z == 0, z == last)

    def ready(j, s, c):
        @pl.when(jnp.logical_and(at_end, j > 0))
        def _():
            w_passed(s, c, flip(z, 1), wr_send).wait_recv()

    def product(q, s, c):
        base = wbuf[s, pl.ds(pl.multiple_of(c * rows, rows), rows)]
        full = lax.dot_general(gbuf[q], base, NT, preferred_element_type=F32)
        route = rq[q]
        total = acc[q]
        for i in range(rows // (2 * rank)):
            expert = (s * experts + c * per_chunk + 2 * i).astype(F32)
            total += jnp.where(route == expert, full[:, i * 2 * rank:(i + 1) * 2 * rank], 0.0)
        return total

    def unit(u, carry):
        j, c = u // CHUNKS, u % CHUNKS
        s = shard_at(j)
        ready(j, s, c)

        def one(q, inner):
            acc[q] = product(q, s, c)
            return inner

        return lax.fori_loop(0, plane, one, carry)

    units = owners * CHUNKS
    lax.fori_loop(0, units - 1, unit, 0)

    s, c = shard_at(last), CHUNKS - 1
    ready(last, s, c)
    low_half = lax.broadcasted_iota(I32, (half_tokens, 2 * rank), 1) < rank

    def finish(r, carry):
        q = (me + r) % plane
        total = product(q, s, c)
        total = jnp.sum(total.reshape(tokens, topk, 2 * rank), axis=1)
        total = total + pltpu.roll(total, rank, 1)
        psend[q] = jnp.where(low_half, total[:half_tokens], total[half_tokens:])

        @pl.when(r < plane)
        def _():
            p_copy(q, r).start()

        return carry

    lax.fori_loop(1, plane + 1, finish, 0)
    right = psend[me]
    for r in range(1, plane):
        p_copy((me + r) % plane, r).wait_recv()
        right += pbuf[(me + plane - r) % plane]
    turned = pltpu.roll(right, rank, 1)
    right = jnp.concatenate(
        [jnp.where(low_half, right, turned), jnp.where(low_half, turned, right)], axis=0
    )
    sketch = (lrep[...] * jnp.tile(right, (1, rank // 2))).astype(BF16)
    out_ref[...] = lax.dot_general(sketch, bsel[...], NT, preferred_element_type=F32)

    for r in range(1, plane):
        g_copy((me + r) % plane, r).wait_send()
        r_copy((me + r) % plane, r).wait_send()
        p_copy((me + r) % plane, r).wait_send()
    for copy in b_copies:
        copy.wait_send()

    def sent(i, carry):
        s, c = i // CHUNKS, i % CHUNKS

        @pl.when(jnp.logical_and(z < last, s <= z))
        def _():
            w_passed(s, c, z + 1, wr_send).wait_send()

        @pl.when(jnp.logical_and(z > 0, s >= z))
        def _():
            w_passed(s, c, z - 1, wl_send).wait_send()

        return carry

    lax.fori_loop(0, units, sent, 0)


def local(inputs, out_grads, routing, in_basis, out_basis, val_bank, val_ids):
    tokens, model = inputs.shape
    topk, hidden = out_grads.shape[1:]
    experts, _, rank = out_basis.shape
    groups, owners, dps = (lax.axis_size(a) for a in ("groups", "expert", "dp"))
    plane = groups * dps
    pairs = tokens * topk
    width = hidden // plane
    flat = val_bank.shape[1]
    count = val_ids.shape[0]
    dma = pltpu.SemaphoreType.DMA
    hbm = pl.BlockSpec(memory_space=pl.ANY)
    vmem = pl.BlockSpec(memory_space=pltpu.VMEM)
    return pl.pallas_call(
        functools.partial(kernel, (groups, owners, dps, topk, experts, rank)),
        out_shape=jax.ShapeDtypeStruct((tokens, count), F32),
        in_specs=[hbm, hbm, hbm, vmem, hbm, hbm, vmem],
        out_specs=vmem,
        scratch_shapes=[
            pltpu.VMEM((tokens, model), BF16),
            pltpu.VMEM((rank, model), BF16),
            pltpu.VMEM((plane, pairs, width), BF16),
            pltpu.VMEM((owners, experts * rank, width), BF16),
            pltpu.VMEM((plane, topk, 128), F32),
            pltpu.VMEM((plane, pairs, 2 * rank), F32),
            pltpu.VMEM((plane, pairs, 2 * rank), F32),
            pltpu.VMEM((plane, tokens // 2, 2 * rank), F32),
            pltpu.VMEM((plane, tokens // 2, 2 * rank), F32),
            pltpu.VMEM((dps,) + val_bank.shape, BF16),
            pltpu.VMEM((count, flat), BF16),
            pltpu.VMEM((tokens, flat), F32),
            dma((plane,)), dma((plane,)), dma((plane,)), dma((plane,)),
            dma((plane,)), dma((plane,)), dma((dps,)), dma((dps,)),
            dma((owners * CHUNKS,)), dma((owners * CHUNKS,)), dma((owners * CHUNKS,)),
            dma((5,)),
        ],
        compiler_params=pltpu.CompilerParams(
            collective_id=0, has_side_effects=True, vmem_limit_bytes=48 * 1024 * 1024
        ),
    )(
        inputs,
        in_basis.T,
        out_grads.reshape(pairs, hidden),
        routing.T,
        out_basis.transpose(0, 2, 1).reshape(experts * rank, hidden),
        val_bank,
        val_ids.reshape(1, count),
    )


def solution(mesh):
    return jax.shard_map(
        local,
        mesh=mesh,
        in_specs=(
            P(("groups", "expert", "dp"), None),
            P(("groups", "expert", "dp"), None, None),
            P(("groups", "expert", "dp"), None),
            P(),
            P("expert", None, None),
            P(("groups", "dp"), None),
            P("groups"),
        ),
        out_specs=P(("groups", "expert", "dp"), None),
        check_vma=False,
    )
```

```python
import functools

import jax
import jax.numpy as jnp
from jax import lax
from jax.experimental import pallas as pl
from jax.experimental.pallas import tpu as pltpu
from jax.sharding import PartitionSpec as P

F32, BF16, I32 = jnp.float32, jnp.bfloat16, jnp.int32
MESH = pl.DeviceIdType.MESH
NT = (((1,), (1,)), ((), ()))
TN = (((0,), (0,)), ((), ()))
CHUNKS = 2


def flip(index, mask):
    result, bit = index, 1
    while bit <= mask:
        if mask & bit:
            result = result + bit * (1 - 2 * ((index // bit) % 2))
        bit *= 2
    return result


def kernel(
    sizes, x_ref, inb_ref, og_ref, rt_ref, wt_ref, bank_ref, ids_ref, out_ref,
    xbuf, ibuf, gbuf, wbuf, rbuf, rq, acc, psend, pbuf, bbuf, bsel, lrep, rt_buf, ids_buf,
    g_send, g_recv, r_send, r_recv, p_send, p_recv, b_send, b_recv,
    wr_send, wl_send, w_recv, local_sem,
):
    groups, owners, dps, topk, experts, rank = sizes
    plane = groups * dps
    tokens = x_ref.shape[0]
    pairs = og_ref.shape[0]
    width = gbuf.shape[2]
    rows = wt_ref.shape[0] // CHUNKS
    half_tokens = tokens // 2
    g, z, d = lax.axis_index("groups"), lax.axis_index("expert"), lax.axis_index("dp")
    me = g * dps + d
    last = owners - 1

    def place(q):
        return {"groups": q // dps, "dp": q % dps}

    barrier = pltpu.get_barrier_semaphore()
    for r in range(1, plane):
        pl.semaphore_signal(barrier, inc=1, device_id=place((me + r) % plane), device_id_type=MESH)

    @pl.when(z > 0)
    def _():
        pl.semaphore_signal(barrier, inc=1, device_id={"expert": z - 1}, device_id_type=MESH)

    @pl.when(z < last)
    def _():
        pl.semaphore_signal(barrier, inc=1, device_id={"expert": z + 1}, device_id_type=MESH)

    def slice_of(q):
        return pl.ds(pl.multiple_of(q * width, width), width)

    local = [
        pltpu.make_async_copy(x_ref, xbuf, local_sem.at[0]),
        pltpu.make_async_copy(inb_ref, ibuf, local_sem.at[1]),
        pltpu.make_async_copy(og_ref.at[:, slice_of(me)], gbuf.at[me], local_sem.at[2]),
        pltpu.make_async_copy(wt_ref.at[:, slice_of(me)], wbuf.at[z], local_sem.at[3]),
        pltpu.make_async_copy(bank_ref, bbuf.at[d], local_sem.at[4]),
    ]
    local = [
        pltpu.make_async_copy(rt_ref, rt_buf, local_sem.at[5]),
        pltpu.make_async_copy(ids_ref, ids_buf, local_sem.at[6]),
    ] + local
    for copy in local:
        copy.start()
    local.pop(0).wait()
    local.pop(0).wait()
    rbuf[me] = jnp.zeros(rbuf.shape[1:], F32)
    rbuf[me, :, :tokens] = rt_buf[...].astype(F32)

    def w_copy(source, s, c, to, sems):
        return pltpu.make_async_remote_copy(
            src_ref=source,
            dst_ref=wbuf.at[s, pl.ds(c * rows, rows)],
            send_sem=sems.at[s * CHUNKS + c],
            recv_sem=w_recv.at[s * CHUNKS + c],
            device_id={"expert": to},
            device_id_type=MESH,
        )

    def w_passed(s, c, to, sems):
        return w_copy(wbuf.at[s, pl.ds(c * rows, rows)], s, c, to, sems)

    def g_copy(q, r):
        return pltpu.make_async_remote_copy(
            src_ref=og_ref.at[:, slice_of(q)], dst_ref=gbuf.at[me],
            send_sem=g_send.at[r], recv_sem=g_recv.at[r],
            device_id=place(q), device_id_type=MESH,
        )

    def r_copy(q, r):
        return pltpu.make_async_remote_copy(
            src_ref=rbuf.at[me], dst_ref=rbuf.at[me],
            send_sem=r_send.at[r], recv_sem=r_recv.at[r],
            device_id=place(q), device_id_type=MESH,
        )

    def p_copy(q, r):
        return pltpu.make_async_remote_copy(
            src_ref=psend.at[q], dst_ref=pbuf.at[me],
            send_sem=p_send.at[r], recv_sem=p_recv.at[r],
            device_id=place(q), device_id_type=MESH,
        )

    bits = []
    bit = dps // 2
    while bit:
        bits.append(bit)
        bit //= 2
    b_copies = []

    def b_copy(source, shard, bit):
        copy = pltpu.make_async_remote_copy(
            src_ref=source, dst_ref=bbuf.at[shard],
            send_sem=b_send.at[len(b_copies)], recv_sem=b_recv.at[shard],
            device_id={"dp": flip(d, bit)}, device_id_type=MESH,
        )
        b_copies.append(copy)
        return copy

    def b_wait(shard):
        pltpu.make_async_remote_copy(
            src_ref=bbuf.at[shard], dst_ref=bbuf.at[shard],
            send_sem=b_send.at[0], recv_sem=b_recv.at[shard],
            device_id={"dp": flip(d, 1)}, device_id_type=MESH,
        ).wait_recv()

    pl.semaphore_wait(barrier, plane - 1 + jnp.where(z > 0, 1, 0) + jnp.where(z < last, 1, 0))

    for c in range(CHUNKS):
        own = wt_ref.at[pl.ds(c * rows, rows), slice_of(me)]

        @pl.when(z > 0)
        def _(own=own, c=c):
            w_copy(own, z, c, z - 1, wl_send).start()

        @pl.when(z < last)
        def _(own=own, c=c):
            w_copy(own, z, c, z + 1, wr_send).start()

    for r in range(1, plane):
        g_copy((me + r) % plane, r).start()
        r_copy((me + r) % plane, r).start()
    for bit in bits:
        b_copy(bank_ref, d, bit).start()

    local[0].wait()
    local[1].wait()
    left = lax.dot_general(xbuf[...], ibuf[...], NT, preferred_element_type=F32)
    left = left.astype(BF16).astype(F32)
    low = lax.broadcasted_iota(I32, (tokens, 2 * rank), 1) < rank
    for i in range(rank // 2):
        lrep[:, i * 2 * rank:(i + 1) * 2 * rank] = jnp.where(
            low, left[:, 2 * i:2 * i + 1], left[:, 2 * i + 1:2 * i + 2]
        )
    acc[...] = jnp.zeros_like(acc)

    @pl.when(jnp.logical_and(z > 0, z < last))
    def _():
        def step(i, carry):
            j, c = i // CHUNKS, i % CHUNKS

            @pl.when(z - 1 - j >= 0)
            def _():
                copy = w_passed(z - 1 - j, c, z + 1, wr_send)
                copy.wait_recv()
                copy.start()

            @pl.when(z + 1 + j <= last)
            def _():
                copy = w_passed(z + 1 + j, c, z - 1, wl_send)
                copy.wait_recv()
                copy.start()

            return carry

        lax.fori_loop(0, (owners - 2) * CHUNKS, step, 0)

    for r in range(1, plane):
        r_copy((me + r) % plane, r).wait_recv()
    shift, mask = topk.bit_length() - 1, topk - 1
    spread = (
        lax.broadcasted_iota(I32, (pairs, rbuf.shape[2]), 0) >> shift
        == lax.broadcasted_iota(I32, (pairs, rbuf.shape[2]), 1)
    ).astype(F32).astype(BF16)
    mine = (
        lax.broadcasted_iota(I32, (pairs, topk), 0) & mask
        == lax.broadcasted_iota(I32, (pairs, topk), 1)
    )
    half = (lax.broadcasted_iota(I32, (pairs, 2 * rank), 1) >= rank).astype(F32)

    def routes(q, carry):
        named = lax.dot_general(spread, rbuf[q].astype(BF16), NT, preferred_element_type=F32)
        named = jnp.sum(jnp.where(mine, named, 0.0), axis=1, keepdims=True)
        rq[q] = named - half
        return carry

    lax.fori_loop(0, plane, routes, 0)

    masks = [m for b in bits for m in range(1, dps) if m & -m == b]
    for m in masks:
        b_wait(flip(d, m))
        for bit in bits:
            if bit < (m & -m):
                b_copy(bbuf.at[flip(d, m)], flip(d, m), bit).start()
    local[4].wait()
    bank_rows = dps * bank_ref.shape[0]
    select = (
        lax.broadcasted_iota(I32, (bank_rows, ids_ref.shape[1]), 0) == ids_buf[...]
    ).astype(F32).astype(BF16)
    cut = 512

    def choose(i, carry):
        columns = pl.ds(pl.multiple_of(i * cut, cut), cut)
        whole = bbuf[:, :, columns].reshape(bank_rows, cut)
        bsel[:, columns] = lax.dot_general(
            select, whole, TN, preferred_element_type=F32
        ).astype(BF16)
        return carry

    lax.fori_loop(0, bsel.shape[1] // cut, choose, 0)

    for r in range(1, plane):
        g_copy((me + r) % plane, r).wait_recv()
    local[2].wait()
    local[3].wait()

    near = jnp.minimum(z, last - z)
    far_sign = jnp.where(z < last - z, 1, -1)

    def shard_at(j):
        paired = j <= 2 * near
        distance = jnp.where(paired, (j + 1) // 2, j - near)
        sign = jnp.where(paired, 1 - 2 * (j % 2), far_sign)
        return z + sign * distance

    at_end = jnp.logical_or(z == 0, z == last)

    def ready(j, s):
        @pl.when(jnp.logical_and(at_end, j > 0))
        def _():
            for c in range(CHUNKS):
                w_passed(s, c, flip(z, 1), wr_send).wait_recv()

    def product(q, s):
        full = lax.dot_general(gbuf[q], wbuf[s], NT, preferred_element_type=F32)
        route = rq[q] - (s * experts).astype(F32)
        total = acc[q]
        for i in range(experts // 2):
            total += jnp.where(route == 2.0 * i, full[:, i * 2 * rank:(i + 1) * 2 * rank], 0.0)
        return total

    def unit(j, carry):
        s = shard_at(j)
        ready(j, s)
        for q in range(plane):
            acc[q] = product(q, s)
        return carry

    lax.fori_loop(0, last, unit, 0)

    s = shard_at(last)
    ready(last, s)
    low_half = lax.broadcasted_iota(I32, (half_tokens, 2 * rank), 1) < rank

    for r in range(1, plane + 1):
        q = (me + r) % plane
        total = product(q, s)
        total = jnp.sum(total.reshape(tokens, topk, 2 * rank), axis=1)
        total = total + pltpu.roll(total, rank, 1)
        psend[q] = jnp.where(low_half, total[:half_tokens], total[half_tokens:])
        if r < plane:
            p_copy(q, r).start()

    right = psend[me]
    for r in range(1, plane):
        p_copy((me + r) % plane, r).wait_recv()
        right += pbuf[(me + plane - r) % plane]
    turned = pltpu.roll(right, rank, 1)
    right = jnp.concatenate(
        [jnp.where(low_half, right, turned), jnp.where(low_half, turned, right)], axis=0
    )
    sketch = (lrep[...] * jnp.tile(right, (1, rank // 2))).astype(BF16)
    out_ref[...] = lax.dot_general(sketch, bsel[...], NT, preferred_element_type=F32)

    for r in range(1, plane):
        g_copy((me + r) % plane, r).wait_send()
        r_copy((me + r) % plane, r).wait_send()
        p_copy((me + r) % plane, r).wait_send()
    for copy in b_copies:
        copy.wait_send()

    def sent(i, carry):
        s, c = i // CHUNKS, i % CHUNKS

        @pl.when(jnp.logical_and(z < last, s <= z))
        def _():
            w_passed(s, c, z + 1, wr_send).wait_send()

        @pl.when(jnp.logical_and(z > 0, s >= z))
        def _():
            w_passed(s, c, z - 1, wl_send).wait_send()

        return carry

    lax.fori_loop(0, owners * CHUNKS, sent, 0)


def local(inputs, out_grads, routing, in_basis, out_basis, val_bank, val_ids):
    tokens, model = inputs.shape
    topk, hidden = out_grads.shape[1:]
    experts, _, rank = out_basis.shape
    groups, owners, dps = (lax.axis_size(a) for a in ("groups", "expert", "dp"))
    plane = groups * dps
    pairs = tokens * topk
    width = hidden // plane
    flat = val_bank.shape[1]
    count = val_ids.shape[0]
    dma = pltpu.SemaphoreType.DMA
    hbm = pl.BlockSpec(memory_space=pltpu.HBM)
    vmem = pl.BlockSpec(memory_space=pltpu.VMEM)
    return pl.pallas_call(
        functools.partial(kernel, (groups, owners, dps, topk, experts, rank)),
        out_shape=jax.ShapeDtypeStruct((tokens, count), F32),
        in_specs=[hbm] * 7,
        out_specs=vmem,
        scratch_shapes=[
            pltpu.VMEM((tokens, model), BF16),
            pltpu.VMEM((rank, model), BF16),
            pltpu.VMEM((plane, pairs, width), BF16),
            pltpu.VMEM((owners, experts * rank, width), BF16),
            pltpu.VMEM((plane, topk, 128), F32),
            pltpu.VMEM((plane, pairs, 2 * rank), F32),
            pltpu.VMEM((plane, pairs, 2 * rank), F32),
            pltpu.VMEM((plane, tokens // 2, 2 * rank), F32),
            pltpu.VMEM((plane, tokens // 2, 2 * rank), F32),
            pltpu.VMEM((dps,) + val_bank.shape, BF16),
            pltpu.VMEM((count, flat), BF16),
            pltpu.VMEM((tokens, flat), F32),
            pltpu.VMEM((topk, tokens), I32),
            pltpu.VMEM((1, count), I32),
            dma((plane,)), dma((plane,)), dma((plane,)), dma((plane,)),
            dma((plane,)), dma((plane,)), dma((dps,)), dma((dps,)),
            dma((owners * CHUNKS,)), dma((owners * CHUNKS,)), dma((owners * CHUNKS,)),
            dma((7,)),
        ],
        compiler_params=pltpu.CompilerParams(
            collective_id=0, has_side_effects=True, vmem_limit_bytes=60 * 1024 * 1024
        ),
    )(
        inputs,
        in_basis.T,
        out_grads.reshape(pairs, hidden),
        routing.T,
        out_basis.transpose(0, 2, 1).reshape(experts * rank, hidden),
        val_bank,
        val_ids.reshape(1, count),
    )


def solution(mesh):
    return jax.shard_map(
        local,
        mesh=mesh,
        in_specs=(
            P(("groups", "expert", "dp"), None),
            P(("groups", "expert", "dp"), None, None),
            P(("groups", "expert", "dp"), None),
            P(),
            P("expert", None, None),
            P(("groups", "dp"), None),
            P("groups"),
        ),
        out_specs=P(("groups", "expert", "dp"), None),
        check_vma=False,
    )
```

```python
import functools

import jax
import jax.numpy as jnp
from jax import lax
from jax.experimental import pallas as pl
from jax.experimental.pallas import tpu as pltpu
from jax.sharding import PartitionSpec as P

F32, BF16, I32 = jnp.float32, jnp.bfloat16, jnp.int32
MESH = pl.DeviceIdType.MESH
NT = (((1,), (1,)), ((), ()))
TN = (((0,), (0,)), ((), ()))
CHUNKS = 2


def flip(index, mask):
    result, bit = index, 1
    while bit <= mask:
        if mask & bit:
            result = result + bit * (1 - 2 * ((index // bit) % 2))
        bit *= 2
    return result


def kernel(
    sizes, x_ref, inb_ref, og_ref, rt_ref, wt_ref, bank_ref, ids_ref, out_ref,
    xbuf, ibuf, gbuf, wbuf, rbuf, rq, acc, psend, pbuf, bbuf, bsel, lrep, rt_buf, ids_buf,
    g_send, g_recv, r_send, r_recv, p_send, p_recv, b_send, b_recv,
    wr_send, wl_send, w_recv, local_sem,
):
    groups, owners, dps, topk, experts, rank = sizes
    plane = groups * dps
    tokens = x_ref.shape[0]
    pairs = og_ref.shape[0]
    width = gbuf.shape[2]
    rows = wt_ref.shape[0] // CHUNKS
    half_tokens = tokens // 2
    g, z, d = lax.axis_index("groups"), lax.axis_index("expert"), lax.axis_index("dp")
    me = g * dps + d
    last = owners - 1

    def place(q):
        return {"groups": q // dps, "dp": q % dps}

    barrier = pltpu.get_barrier_semaphore()
    for r in range(1, plane):
        pl.semaphore_signal(barrier, inc=1, device_id=place((me + r) % plane), device_id_type=MESH)

    @pl.when(z > 0)
    def _():
        pl.semaphore_signal(barrier, inc=1, device_id={"expert": z - 1}, device_id_type=MESH)

    @pl.when(z < last)
    def _():
        pl.semaphore_signal(barrier, inc=1, device_id={"expert": z + 1}, device_id_type=MESH)

    def slice_of(q):
        return pl.ds(pl.multiple_of(q * width, width), width)

    local = [
        pltpu.make_async_copy(x_ref, xbuf, local_sem.at[0]),
        pltpu.make_async_copy(inb_ref, ibuf, local_sem.at[1]),
        pltpu.make_async_copy(og_ref.at[:, slice_of(me)], gbuf.at[me], local_sem.at[2]),
        pltpu.make_async_copy(wt_ref.at[:, slice_of(me)], wbuf.at[z], local_sem.at[3]),
        pltpu.make_async_copy(bank_ref, bbuf.at[d], local_sem.at[4]),
    ]
    local = [
        pltpu.make_async_copy(rt_ref, rt_buf, local_sem.at[5]),
        pltpu.make_async_copy(ids_ref, ids_buf, local_sem.at[6]),
    ] + local
    for copy in local:
        copy.start()
    local.pop(0).wait()
    local.pop(0).wait()
    rbuf[me] = jnp.zeros(rbuf.shape[1:], F32)
    rbuf[me, :, :tokens] = rt_buf[...].astype(F32)

    def w_copy(source, s, c, to, sems):
        return pltpu.make_async_remote_copy(
            src_ref=source,
            dst_ref=wbuf.at[s, pl.ds(c * rows, rows)],
            send_sem=sems.at[s * CHUNKS + c],
            recv_sem=w_recv.at[s * CHUNKS + c],
            device_id={"expert": to},
            device_id_type=MESH,
        )

    def w_passed(s, c, to, sems):
        return w_copy(wbuf.at[s, pl.ds(c * rows, rows)], s, c, to, sems)

    def g_copy(q, r):
        return pltpu.make_async_remote_copy(
            src_ref=og_ref.at[:, slice_of(q)], dst_ref=gbuf.at[me],
            send_sem=g_send.at[r], recv_sem=g_recv.at[r],
            device_id=place(q), device_id_type=MESH,
        )

    def r_copy(q, r):
        return pltpu.make_async_remote_copy(
            src_ref=rbuf.at[me], dst_ref=rbuf.at[me],
            send_sem=r_send.at[r], recv_sem=r_recv.at[r],
            device_id=place(q), device_id_type=MESH,
        )

    def p_copy(q, r):
        return pltpu.make_async_remote_copy(
            src_ref=psend.at[q], dst_ref=pbuf.at[me],
            send_sem=p_send.at[r], recv_sem=p_recv.at[r],
            device_id=place(q), device_id_type=MESH,
        )

    bits = []
    bit = dps // 2
    while bit:
        bits.append(bit)
        bit //= 2
    b_copies = []

    def b_copy(source, shard, bit):
        copy = pltpu.make_async_remote_copy(
            src_ref=source, dst_ref=bbuf.at[shard],
            send_sem=b_send.at[len(b_copies)], recv_sem=b_recv.at[shard],
            device_id={"dp": flip(d, bit)}, device_id_type=MESH,
        )
        b_copies.append(copy)
        return copy

    def b_wait(shard):
        pltpu.make_async_remote_copy(
            src_ref=bbuf.at[shard], dst_ref=bbuf.at[shard],
            send_sem=b_send.at[0], recv_sem=b_recv.at[shard],
            device_id={"dp": flip(d, 1)}, device_id_type=MESH,
        ).wait_recv()

    pl.semaphore_wait(barrier, plane - 1 + jnp.where(z > 0, 1, 0) + jnp.where(z < last, 1, 0))

    for c in range(CHUNKS):
        own = wt_ref.at[pl.ds(c * rows, rows), slice_of(me)]

        @pl.when(z > 0)
        def _(own=own, c=c):
            w_copy(own, z, c, z - 1, wl_send).start()

        @pl.when(z < last)
        def _(own=own, c=c):
            w_copy(own, z, c, z + 1, wr_send).start()

    for r in range(1, plane):
        g_copy((me + r) % plane, r).start()
        r_copy((me + r) % plane, r).start()
    for bit in bits:
        b_copy(bank_ref, d, bit).start()

    local[0].wait()
    local[1].wait()
    left = lax.dot_general(xbuf[...], ibuf[...], NT, preferred_element_type=F32)
    left = left.astype(BF16).astype(F32)
    low = lax.broadcasted_iota(I32, (tokens, 2 * rank), 1) < rank
    for i in range(rank // 2):
        lrep[:, i * 2 * rank:(i + 1) * 2 * rank] = jnp.where(
            low, left[:, 2 * i:2 * i + 1], left[:, 2 * i + 1:2 * i + 2]
        )
    acc[...] = jnp.zeros_like(acc)

    @pl.when(jnp.logical_and(z > 0, z < last))
    def _():
        def step(i, carry):
            j, c = i // CHUNKS, i % CHUNKS

            @pl.when(z - 1 - j >= 0)
            def _():
                copy = w_passed(z - 1 - j, c, z + 1, wr_send)
                copy.wait_recv()
                copy.start()

            @pl.when(z + 1 + j <= last)
            def _():
                copy = w_passed(z + 1 + j, c, z - 1, wl_send)
                copy.wait_recv()
                copy.start()

            return carry

        lax.fori_loop(0, (owners - 2) * CHUNKS, step, 0)

    for r in range(1, plane):
        r_copy((me + r) % plane, r).wait_recv()
    shift, mask = topk.bit_length() - 1, topk - 1
    spread = (
        lax.broadcasted_iota(I32, (pairs, rbuf.shape[2]), 0) >> shift
        == lax.broadcasted_iota(I32, (pairs, rbuf.shape[2]), 1)
    ).astype(F32).astype(BF16)
    mine = (
        lax.broadcasted_iota(I32, (pairs, topk), 0) & mask
        == lax.broadcasted_iota(I32, (pairs, topk), 1)
    )
    half = (lax.broadcasted_iota(I32, (pairs, 2 * rank), 1) >= rank).astype(F32)

    def routes(q, carry):
        named = lax.dot_general(spread, rbuf[q].astype(BF16), NT, preferred_element_type=F32)
        named = jnp.sum(jnp.where(mine, named, 0.0), axis=1, keepdims=True)
        rq[q] = named - half
        return carry

    lax.fori_loop(0, plane, routes, 0)

    near = jnp.minimum(z, last - z)
    far_sign = jnp.where(z < last - z, 1, -1)

    def shard_at(j):
        paired = j <= 2 * near
        distance = jnp.where(paired, (j + 1) // 2, j - near)
        sign = jnp.where(paired, 1 - 2 * (j % 2), far_sign)
        return z + sign * distance

    at_end = jnp.logical_or(z == 0, z == last)

    def ready(j, s):
        @pl.when(jnp.logical_and(at_end, j > 0))
        def _():
            for c in range(CHUNKS):
                w_passed(s, c, flip(z, 1), wr_send).wait_recv()

    def product(q, s):
        full = lax.dot_general(gbuf[q], wbuf[s], NT, preferred_element_type=F32)
        route = rq[q] - (s * experts).astype(F32)
        total = acc[q]
        for i in range(experts // 2):
            total += jnp.where(route == 2.0 * i, full[:, i * 2 * rank:(i + 1) * 2 * rank], 0.0)
        return total

    def unit(j, carry):
        s = shard_at(j)
        ready(j, s)
        for q in range(plane):
            acc[q] = product(q, s)
        return carry

    local[2].wait()
    local[3].wait()
    for r in range(plane):
        if r:
            g_copy((me + r) % plane, r).wait_recv()
        q = (me + plane - r) % plane
        acc[q] = product(q, z)
    lax.fori_loop(1, last, unit, 0)

    masks = [m for b in bits for m in range(1, dps) if m & -m == b]
    for m in masks:
        if m & -m > 1:
            b_wait(flip(d, m))
            for bit in bits:
                if bit < (m & -m):
                    b_copy(bbuf.at[flip(d, m)], flip(d, m), bit).start()

    s = shard_at(last)
    ready(last, s)
    low_half = lax.broadcasted_iota(I32, (half_tokens, 2 * rank), 1) < rank

    for r in range(1, plane + 1):
        q = (me + r) % plane
        total = product(q, s)
        total = jnp.sum(total.reshape(tokens, topk, 2 * rank), axis=1)
        total = total + pltpu.roll(total, rank, 1)
        psend[q] = jnp.where(low_half, total[:half_tokens], total[half_tokens:])
        if r < plane:
            p_copy(q, r).start()

    for m in masks:
        if m & -m == 1:
            b_wait(flip(d, m))
    local[4].wait()
    bank_rows = dps * bank_ref.shape[0]
    select = (
        lax.broadcasted_iota(I32, (bank_rows, ids_ref.shape[1]), 0) == ids_buf[...]
    ).astype(F32).astype(BF16)
    cut = 512

    def choose(i, carry):
        columns = pl.ds(pl.multiple_of(i * cut, cut), cut)
        whole = bbuf[:, :, columns].reshape(bank_rows, cut)
        bsel[:, columns] = lax.dot_general(
            select, whole, TN, preferred_element_type=F32
        ).astype(BF16)
        return carry

    lax.fori_loop(0, bsel.shape[1] // cut, choose, 0)


    right = psend[me]
    for r in range(1, plane):
        p_copy((me + r) % plane, r).wait_recv()
        right += pbuf[(me + plane - r) % plane]
    turned = pltpu.roll(right, rank, 1)
    right = jnp.concatenate(
        [jnp.where(low_half, right, turned), jnp.where(low_half, turned, right)], axis=0
    )
    sketch = (lrep[...] * jnp.tile(right, (1, rank // 2))).astype(BF16)
    out_ref[...] = lax.dot_general(sketch, bsel[...], NT, preferred_element_type=F32)

    for r in range(1, plane):
        g_copy((me + r) % plane, r).wait_send()
        r_copy((me + r) % plane, r).wait_send()
        p_copy((me + r) % plane, r).wait_send()
    for copy in b_copies:
        copy.wait_send()

    def sent(i, carry):
        s, c = i // CHUNKS, i % CHUNKS

        @pl.when(jnp.logical_and(z < last, s <= z))
        def _():
            w_passed(s, c, z + 1, wr_send).wait_send()

        @pl.when(jnp.logical_and(z > 0, s >= z))
        def _():
            w_passed(s, c, z - 1, wl_send).wait_send()

        return carry

    lax.fori_loop(0, owners * CHUNKS, sent, 0)


def local(inputs, out_grads, routing, in_basis, out_basis, val_bank, val_ids):
    tokens, model = inputs.shape
    topk, hidden = out_grads.shape[1:]
    experts, _, rank = out_basis.shape
    groups, owners, dps = (lax.axis_size(a) for a in ("groups", "expert", "dp"))
    plane = groups * dps
    pairs = tokens * topk
    width = hidden // plane
    flat = val_bank.shape[1]
    count = val_ids.shape[0]
    dma = pltpu.SemaphoreType.DMA
    hbm = pl.BlockSpec(memory_space=pltpu.HBM)
    vmem = pl.BlockSpec(memory_space=pltpu.VMEM)
    return pl.pallas_call(
        functools.partial(kernel, (groups, owners, dps, topk, experts, rank)),
        out_shape=jax.ShapeDtypeStruct((tokens, count), F32),
        in_specs=[hbm] * 7,
        out_specs=vmem,
        scratch_shapes=[
            pltpu.VMEM((tokens, model), BF16),
            pltpu.VMEM((rank, model), BF16),
            pltpu.VMEM((plane, pairs, width), BF16),
            pltpu.VMEM((owners, experts * rank, width), BF16),
            pltpu.VMEM((plane, topk, 128), F32),
            pltpu.VMEM((plane, pairs, 2 * rank), F32),
            pltpu.VMEM((plane, pairs, 2 * rank), F32),
            pltpu.VMEM((plane, tokens // 2, 2 * rank), F32),
            pltpu.VMEM((plane, tokens // 2, 2 * rank), F32),
            pltpu.VMEM((dps,) + val_bank.shape, BF16),
            pltpu.VMEM((count, flat), BF16),
            pltpu.VMEM((tokens, flat), F32),
            pltpu.VMEM((topk, tokens), I32),
            pltpu.VMEM((1, count), I32),
            dma((plane,)), dma((plane,)), dma((plane,)), dma((plane,)),
            dma((plane,)), dma((plane,)), dma((dps,)), dma((dps,)),
            dma((owners * CHUNKS,)), dma((owners * CHUNKS,)), dma((owners * CHUNKS,)),
            dma((7,)),
        ],
        compiler_params=pltpu.CompilerParams(
            collective_id=0, has_side_effects=True, vmem_limit_bytes=60 * 1024 * 1024
        ),
    )(
        inputs,
        in_basis.T,
        out_grads.reshape(pairs, hidden),
        routing.T,
        out_basis.transpose(0, 2, 1).reshape(experts * rank, hidden),
        val_bank,
        val_ids.reshape(1, count),
    )


def solution(mesh):
    return jax.shard_map(
        local,
        mesh=mesh,
        in_specs=(
            P(("groups", "expert", "dp"), None),
            P(("groups", "expert", "dp"), None, None),
            P(("groups", "expert", "dp"), None),
            P(),
            P("expert", None, None),
            P(("groups", "dp"), None),
            P("groups"),
        ),
        out_specs=P(("groups", "expert", "dp"), None),
        check_vma=False,
    )
```

```python
import functools

import jax
import jax.numpy as jnp
from jax import lax
from jax.experimental import pallas as pl
from jax.experimental.pallas import tpu as pltpu
from jax.sharding import PartitionSpec as P

F32, BF16, I32 = jnp.float32, jnp.bfloat16, jnp.int32
MESH = pl.DeviceIdType.MESH
NT = (((1,), (1,)), ((), ()))
TN = (((0,), (0,)), ((), ()))
CHUNKS = 2


def flip(index, mask):
    result, bit = index, 1
    while bit <= mask:
        if mask & bit:
            result = result + bit * (1 - 2 * ((index // bit) % 2))
        bit *= 2
    return result


def kernel(
    sizes, x_ref, inb_ref, og_ref, rt_ref, wt_ref, bank_ref, ids_ref, out_ref,
    xbuf, ibuf, gbuf, wbuf, rbuf, rq, acc, psend, pbuf, bbuf, bsel, lrep, rt_buf, ids_buf,
    g_send, g_recv, r_send, r_recv, p_send, p_recv, b_send, b_recv,
    wr_send, wl_send, w_recv, local_sem,
):
    groups, owners, dps, topk, experts, rank = sizes
    plane = groups * dps
    tokens = x_ref.shape[0]
    pairs = og_ref.shape[0]
    width = gbuf.shape[2]
    quarter = wt_ref.shape[0] // 4
    bounds = ((0, 2 * quarter), (2 * quarter, 4 * quarter))
    half_tokens = tokens // 2
    g, z, d = lax.axis_index("groups"), lax.axis_index("expert"), lax.axis_index("dp")
    me = g * dps + d
    last = owners - 1

    def place(q):
        return {"groups": q // dps, "dp": q % dps}

    barrier = pltpu.get_barrier_semaphore()
    for r in range(1, plane):
        pl.semaphore_signal(barrier, inc=1, device_id=place((me + r) % plane), device_id_type=MESH)

    @pl.when(z > 0)
    def _():
        pl.semaphore_signal(barrier, inc=1, device_id={"expert": z - 1}, device_id_type=MESH)

    @pl.when(z < last)
    def _():
        pl.semaphore_signal(barrier, inc=1, device_id={"expert": z + 1}, device_id_type=MESH)

    def slice_of(q):
        return pl.ds(pl.multiple_of(q * width, width), width)

    local = [
        pltpu.make_async_copy(x_ref, xbuf, local_sem.at[0]),
        pltpu.make_async_copy(inb_ref, ibuf, local_sem.at[1]),
        pltpu.make_async_copy(og_ref.at[:, slice_of(me)], gbuf.at[me], local_sem.at[2]),
        pltpu.make_async_copy(wt_ref.at[:, slice_of(me)], wbuf.at[z], local_sem.at[3]),
        pltpu.make_async_copy(bank_ref, bbuf.at[d], local_sem.at[4]),
    ]
    local = [
        pltpu.make_async_copy(rt_ref, rt_buf, local_sem.at[5]),
        pltpu.make_async_copy(ids_ref, ids_buf, local_sem.at[6]),
    ] + local
    for copy in local:
        copy.start()
    local.pop(0).wait()
    local.pop(0).wait()
    rbuf[me] = jnp.zeros(rbuf.shape[1:], F32)
    rbuf[me, :, :tokens] = rt_buf[...].astype(F32)

    def part(c):
        return pl.ds(bounds[c][0], bounds[c][1] - bounds[c][0])

    def w_copy(source, s, c, to, sems):
        return pltpu.make_async_remote_copy(
            src_ref=source,
            dst_ref=wbuf.at[s, part(c)],
            send_sem=sems.at[s * CHUNKS + c],
            recv_sem=w_recv.at[s * CHUNKS + c],
            device_id={"expert": to},
            device_id_type=MESH,
        )

    def w_passed(s, c, to, sems):
        return w_copy(wbuf.at[s, part(c)], s, c, to, sems)

    def g_copy(q, r):
        return pltpu.make_async_remote_copy(
            src_ref=og_ref.at[:, slice_of(q)], dst_ref=gbuf.at[me],
            send_sem=g_send.at[r], recv_sem=g_recv.at[r],
            device_id=place(q), device_id_type=MESH,
        )

    def r_copy(q, r):
        return pltpu.make_async_remote_copy(
            src_ref=rbuf.at[me], dst_ref=rbuf.at[me],
            send_sem=r_send.at[r], recv_sem=r_recv.at[r],
            device_id=place(q), device_id_type=MESH,
        )

    def p_copy(q, r):
        return pltpu.make_async_remote_copy(
            src_ref=psend.at[q], dst_ref=pbuf.at[me],
            send_sem=p_send.at[r], recv_sem=p_recv.at[r],
            device_id=place(q), device_id_type=MESH,
        )

    bits = []
    bit = dps // 2
    while bit:
        bits.append(bit)
        bit //= 2
    b_copies = []

    def b_copy(source, shard, bit):
        copy = pltpu.make_async_remote_copy(
            src_ref=source, dst_ref=bbuf.at[shard],
            send_sem=b_send.at[len(b_copies)], recv_sem=b_recv.at[shard],
            device_id={"dp": flip(d, bit)}, device_id_type=MESH,
        )
        b_copies.append(copy)
        return copy

    def b_wait(shard):
        pltpu.make_async_remote_copy(
            src_ref=bbuf.at[shard], dst_ref=bbuf.at[shard],
            send_sem=b_send.at[0], recv_sem=b_recv.at[shard],
            device_id={"dp": flip(d, 1)}, device_id_type=MESH,
        ).wait_recv()

    pl.semaphore_wait(barrier, plane - 1 + jnp.where(z > 0, 1, 0) + jnp.where(z < last, 1, 0))

    for r in range(1, plane):
        r_copy((me + r) % plane, r).start()

    for c in range(CHUNKS):
        own = wt_ref.at[part(c), slice_of(me)]

        @pl.when(z > 0)
        def _(own=own, c=c):
            w_copy(own, z, c, z - 1, wl_send).start()

        @pl.when(z < last)
        def _(own=own, c=c):
            w_copy(own, z, c, z + 1, wr_send).start()

    for r in range(1, plane):
        g_copy((me + r) % plane, r).start()
    for bit in bits:
        b_copy(bank_ref, d, bit).start()

    local[0].wait()
    local[1].wait()
    left = lax.dot_general(xbuf[...], ibuf[...], NT, preferred_element_type=F32)
    left = left.astype(BF16).astype(F32)
    low = lax.broadcasted_iota(I32, (tokens, 2 * rank), 1) < rank
    for i in range(rank // 2):
        lrep[:, i * 2 * rank:(i + 1) * 2 * rank] = jnp.where(
            low, left[:, 2 * i:2 * i + 1], left[:, 2 * i + 1:2 * i + 2]
        )

    @pl.when(jnp.logical_and(z > 0, z < last))
    def _():
        def step(j, carry):
            for c in range(CHUNKS):

                @pl.when(z - 1 - j >= 0)
                def _(c=c):
                    copy = w_passed(z - 1 - j, c, z + 1, wr_send)
                    copy.wait_recv()
                    copy.start()

                @pl.when(z + 1 + j <= last)
                def _(c=c):
                    copy = w_passed(z + 1 + j, c, z - 1, wl_send)
                    copy.wait_recv()
                    copy.start()

            return carry

        lax.fori_loop(0, owners - 2, step, 0)

    for r in range(1, plane):
        r_copy((me + r) % plane, r).wait_recv()
    shift, mask = topk.bit_length() - 1, topk - 1
    spread = (
        lax.broadcasted_iota(I32, (pairs, rbuf.shape[2]), 0) >> shift
        == lax.broadcasted_iota(I32, (pairs, rbuf.shape[2]), 1)
    ).astype(F32).astype(BF16)
    mine = (
        lax.broadcasted_iota(I32, (pairs, topk), 0) & mask
        == lax.broadcasted_iota(I32, (pairs, topk), 1)
    )
    half = (lax.broadcasted_iota(I32, (pairs, 2 * rank), 1) >= rank).astype(F32)

    def routes(q, carry):
        named = lax.dot_general(spread, rbuf[q].astype(BF16), NT, preferred_element_type=F32)
        named = jnp.sum(jnp.where(mine, named, 0.0), axis=1, keepdims=True)
        rq[q] = named - half
        return carry

    lax.fori_loop(0, plane, routes, 0)

    near = jnp.minimum(z, last - z)
    far_sign = jnp.where(z < last - z, 1, -1)

    def shard_at(j):
        paired = j <= 2 * near
        distance = jnp.where(paired, (j + 1) // 2, j - near)
        sign = jnp.where(paired, 1 - 2 * (j % 2), far_sign)
        return z + sign * distance

    at_end = jnp.logical_or(z == 0, z == last)

    def ready(j, s, c):
        @pl.when(jnp.logical_and(at_end, j > 0))
        def _():
            w_passed(s, c, flip(z, 1), wr_send).wait_recv()

    def product(q, s, total, start, stop):
        full = lax.dot_general(gbuf[q], wbuf[s, start:stop], NT, preferred_element_type=F32)
        route = rq[q] - (s * experts + start // rank).astype(F32)
        for i in range((stop - start) // (2 * rank)):
            total += jnp.where(route == 2.0 * i, full[:, i * 2 * rank:(i + 1) * 2 * rank], 0.0)
        return total

    local[2].wait()
    local[3].wait()

    def arrived(j, carry):
        for c in range(CHUNKS):
            ready(j, shard_at(j), c)
        return carry

    lax.fori_loop(0, last, arrived, 0)
    for r in range(plane):
        if r:
            g_copy((me + r) % plane, r).wait_recv()
        q = (me + plane - r) % plane

        def with_shard(j, total, q=q):
            return product(q, shard_at(j), total, 0, 4 * quarter)

        total = jnp.zeros(acc.shape[1:], F32)
        if owners <= 4:
            for j in range(last):
                total = with_shard(j, total)
        else:
            total = lax.fori_loop(0, last, with_shard, total)
        acc[q] = total

    masks = [m for b in bits for m in range(1, dps) if m & -m == b]
    for m in masks:
        if m & -m > 1:
            b_wait(flip(d, m))
            for bit in bits:
                if bit < (m & -m):
                    b_copy(bbuf.at[flip(d, m)], flip(d, m), bit).start()

    s = shard_at(last)
    ready(last, s, 0)
    for q in range(plane):
        acc[q] = product(q, s, acc[q], *bounds[0])
    ready(last, s, 1)
    low_half = lax.broadcasted_iota(I32, (half_tokens, 2 * rank), 1) < rank

    for r in range(1, plane + 1):
        q = (me + r) % plane
        total = product(q, s, acc[q], *bounds[1])
        total = jnp.sum(total.reshape(tokens, topk, 2 * rank), axis=1)
        total = total + pltpu.roll(total, rank, 1)
        psend[q] = jnp.where(low_half, total[:half_tokens], total[half_tokens:])
        if r < plane:
            p_copy(q, r).start()

    for m in masks:
        if m & -m == 1:
            b_wait(flip(d, m))
    local[4].wait()
    bank_rows = dps * bank_ref.shape[0]
    select = (
        lax.broadcasted_iota(I32, (bank_rows, ids_ref.shape[1]), 0) == ids_buf[...]
    ).astype(F32).astype(BF16)
    cut = 512

    def choose(i, carry):
        columns = pl.ds(pl.multiple_of(i * cut, cut), cut)
        whole = bbuf[:, :, columns].reshape(bank_rows, cut)
        bsel[:, columns] = lax.dot_general(
            select, whole, TN, preferred_element_type=F32
        ).astype(BF16)
        return carry

    lax.fori_loop(0, bsel.shape[1] // cut, choose, 0)


    right = psend[me]
    for r in range(1, plane):
        p_copy((me + r) % plane, r).wait_recv()
        right += pbuf[(me + plane - r) % plane]
    turned = pltpu.roll(right, rank, 1)
    right = jnp.concatenate(
        [jnp.where(low_half, right, turned), jnp.where(low_half, turned, right)], axis=0
    )
    sketch = (lrep[...] * jnp.tile(right, (1, rank // 2))).astype(BF16)
    out_ref[...] = lax.dot_general(sketch, bsel[...], NT, preferred_element_type=F32)

    for r in range(1, plane):
        g_copy((me + r) % plane, r).wait_send()
        r_copy((me + r) % plane, r).wait_send()
        p_copy((me + r) % plane, r).wait_send()
    for copy in b_copies:
        copy.wait_send()

    def sent(s, carry):
        for c in range(CHUNKS):

            @pl.when(jnp.logical_and(z < last, s <= z))
            def _(c=c):
                w_passed(s, c, z + 1, wr_send).wait_send()

            @pl.when(jnp.logical_and(z > 0, s >= z))
            def _(c=c):
                w_passed(s, c, z - 1, wl_send).wait_send()

        return carry

    lax.fori_loop(0, owners, sent, 0)


def local(inputs, out_grads, routing, in_basis, out_basis, val_bank, val_ids):
    tokens, model = inputs.shape
    topk, hidden = out_grads.shape[1:]
    experts, _, rank = out_basis.shape
    groups, owners, dps = (lax.axis_size(a) for a in ("groups", "expert", "dp"))
    plane = groups * dps
    pairs = tokens * topk
    width = hidden // plane
    flat = val_bank.shape[1]
    count = val_ids.shape[0]
    dma = pltpu.SemaphoreType.DMA
    hbm = pl.BlockSpec(memory_space=pltpu.HBM)
    vmem = pl.BlockSpec(memory_space=pltpu.VMEM)
    return pl.pallas_call(
        functools.partial(kernel, (groups, owners, dps, topk, experts, rank)),
        out_shape=jax.ShapeDtypeStruct((tokens, count), F32),
        in_specs=[hbm] * 7,
        out_specs=vmem,
        scratch_shapes=[
            pltpu.VMEM((tokens, model), BF16),
            pltpu.VMEM((rank, model), BF16),
            pltpu.VMEM((plane, pairs, width), BF16),
            pltpu.VMEM((owners, experts * rank, width), BF16),
            pltpu.VMEM((plane, topk, 128), F32),
            pltpu.VMEM((plane, pairs, 2 * rank), F32),
            pltpu.VMEM((plane, pairs, 2 * rank), F32),
            pltpu.VMEM((plane, tokens // 2, 2 * rank), F32),
            pltpu.VMEM((plane, tokens // 2, 2 * rank), F32),
            pltpu.VMEM((dps,) + val_bank.shape, BF16),
            pltpu.VMEM((count, flat), BF16),
            pltpu.VMEM((tokens, flat), F32),
            pltpu.VMEM((topk, tokens), I32),
            pltpu.VMEM((1, count), I32),
            dma((plane,)), dma((plane,)), dma((plane,)), dma((plane,)),
            dma((plane,)), dma((plane,)), dma((dps,)), dma((dps,)),
            dma((owners * CHUNKS,)), dma((owners * CHUNKS,)), dma((owners * CHUNKS,)),
            dma((7,)),
        ],
        compiler_params=pltpu.CompilerParams(
            collective_id=0, has_side_effects=True, vmem_limit_bytes=60 * 1024 * 1024
        ),
    )(
        inputs,
        in_basis.T,
        out_grads.reshape(pairs, hidden),
        routing.T,
        out_basis.transpose(0, 2, 1).reshape(experts * rank, hidden),
        val_bank,
        val_ids.reshape(1, count),
    )


def solution(mesh):
    return jax.shard_map(
        local,
        mesh=mesh,
        in_specs=(
            P(("groups", "expert", "dp"), None),
            P(("groups", "expert", "dp"), None, None),
            P(("groups", "expert", "dp"), None),
            P(),
            P("expert", None, None),
            P(("groups", "dp"), None),
            P("groups"),
        ),
        out_specs=P(("groups", "expert", "dp"), None),
        check_vma=False,
    )
```
